32 devices in a mesh: row: 2 (over x), col: 4 (over y, core), depth: 4 (over z).
Axes of the slice: x: 2, y: 2, z: 4, core: 2. Of those that a mesh axis runs over, the one named last changes fastest.
Arguments:
- grad_partial: bfloat16 [4, 8192, 8192], P('depth', 'row', 'col'), may hold values from -6 to 6
- grad_scale: float32 [4, 64, 8192], P('depth', 'row', 'col'), may hold values from 0.01 to 3
- momentum: float32 [8192, 8192], P('row', ('col', 'depth')), may hold values from -6 to 6
Outputs:
- new_momentum: float32 [8192, 8192], P('row', ('col', 'depth'))
- update: float32 [8192, 8192], P('row', ('col', 'depth'))
The draws below stay inside these ranges and needn't reach their ends.
All inputs are finite; a program needn't handle non-finite values.
Results may differ from the reference program's by a relative error of at most 0.023.
Values may be sent and summed in bfloat16 or wider, within the bound.
A program may use at most 192 MiB of HBM per device.

```python
import math
import jax
import jax.numpy as jnp
from jax import lax

M = 8192
QBLOCK = 128
PARTIALS = 4
PIECE = 128


def draw_grad_scale(key, part):
    key = jax.random.fold_in(key, 7)
    blocks = M // QBLOCK
    ramp = 3.0 ** (jnp.arange(blocks, dtype=jnp.float32) / max(blocks - 1, 1))
    noise = jnp.exp(jax.random.uniform(key, (PARTIALS, blocks, M), jnp.float32, math.log(0.1), math.log(1.0)))
    return noise * ramp[None, :, None]


def raised(result, own_key, source, target, parts, factor):
    owner, partner = [(jnp.arange(result.shape[position]) // (result.shape[position] // parts)).reshape([-1 if axis == position else 1 for axis in range(result.ndim)]) for position in (source, target)]
    chosen = jax.random.permutation(own_key, parts)[partner]
    strong = (owner == chosen) | (owner == (partner + parts // 2) % parts)
    return jnp.where(strong, factor * result, result)


def levels(key, dims, split, smallest, largest):
    gain = 1.0
    for dim, blocks in split:
        draws = jax.random.uniform(jax.random.fold_in(jax.random.fold_in(key, 6), dim), (blocks,), jnp.float32, smallest / len(split), largest / len(split))
        gain = gain * jnp.repeat(jnp.exp(draws), dims[dim] // blocks).reshape((-1,) + (1,) * (len(dims) - 1 - dim))
    return gain


def normal_values(own_key, shape, scale, bound, pieces=(), kind=jnp.bfloat16):
    drawn = scale * jax.random.normal(own_key, shape, jnp.float32)
    if pieces:
        drawn = drawn * levels(own_key, shape, pieces, -0.22, 0.18)
    return jnp.clip(drawn, -bound, bound).astype(kind)


def gaussian_with(stream_key, shape, deviation, bound, pieces, heavy, held_as=jnp.bfloat16):
    values = deviation * jax.random.normal(stream_key, shape, jnp.float32)
    if pieces:
        values = values * levels(stream_key, shape, pieces, -0.22, 0.18)
    return jnp.clip(raised(values, jax.random.fold_in(stream_key, 3), *heavy), -bound, bound).astype(held_as)


def setup_inputs(seed: int = 0) -> dict:
    key_list = jax.random.split(jax.random.key(seed), 4)
    grad_partial = gaussian_with(key_list[0], (PARTIALS, M, M), 1.0, 6.0, ((0, 4), (1, 2), (2, 4)), (0, 2, 4, 2.0))
    grad_scale = draw_grad_scale(jax.random.fold_in(key_list[3], 71), 0)
    momentum = normal_values(key_list[2], (M, M), 1.0, 6.0, ((0, 2), (1, 16)), jnp.float32)
    return {"grad_partial": grad_partial, "grad_scale": grad_scale, "momentum": momentum}


BETA = 0.95
EPSILON = 1e-07

def reference(grad_partial, grad_scale, momentum):
    groups = M // QBLOCK
    quant_values = grad_partial.astype(jnp.float32).reshape(PARTIALS, groups, QBLOCK, M)
    gradient = lax.optimization_barrier(jnp.sum((quant_values * grad_scale[:, :, None, :]).reshape(PARTIALS, M, M), axis=0))
    new_momentum = BETA * momentum + gradient
    nesterov = gradient + BETA * new_momentum
    total_sq = jnp.sum(nesterov * nesterov)
    ortho_input = (nesterov * (math.sqrt(M) / (1.5 * (jnp.sqrt(total_sq) + EPSILON)))).astype(jnp.bfloat16)
    grouped = ortho_input.reshape(M, M // (PARTIALS * PIECE), PARTIALS, PIECE)

    def add_part(running, index):
        columns = lax.dynamic_index_in_dim(grouped, index, 2, keepdims=False).reshape(M, M // PARTIALS)
        term = lax.dot_general(columns, columns, (((1,), (1,)), ((), ())), preferred_element_type=jnp.float32)
        rounded = lax.optimization_barrier(term.astype(jnp.bfloat16)).astype(jnp.float32)
        return (running + rounded, None)
    gram_sum, unused_out = lax.scan(add_part, jnp.zeros((M, M), jnp.float32), jnp.arange(PARTIALS, dtype=jnp.int32))
    gram_matrix = gram_sum.astype(jnp.bfloat16)
    product = jnp.dot(gram_matrix, ortho_input, preferred_element_type=jnp.float32)
    update = math.sqrt(M) * (1.5 * ortho_input.astype(jnp.float32) - 0.5 * product)
    return (new_momentum, update)
```

```python
import math

import jax
import jax.numpy as jnp
from jax import lax
from jax.sharding import PartitionSpec as P

M = 8192
BETA = 0.95
EPSILON = 1e-07
PIECES = 4


def row_sum(block):
    if lax.axis_size("row") != 2:
        return lax.psum(block.astype(jnp.bfloat16), "row").astype(jnp.float32)
    moved = lax.ppermute(block.astype(jnp.bfloat16), "row", [(0, 1), (1, 0)])
    return block.astype(jnp.float32) + moved.astype(jnp.float32)


def body(grad_partial, grad_scale, momentum):
    depth_count = lax.axis_size("depth")
    rows_blk, cols_blk = grad_partial.shape[1:]
    share = cols_blk // depth_count
    width = share // PIECES
    groups = grad_scale.shape[1]
    group_rows = rows_blk // groups

    def scaled_piece(start):
        quant = lax.slice_in_dim(grad_partial[0], start, start + width, axis=1)
        scale = lax.slice_in_dim(grad_scale[0], start, start + width, axis=1)
        quant = quant.astype(jnp.float32).reshape(groups, group_rows, width)
        return (quant * scale[:, None, :]).reshape(rows_blk, width).astype(jnp.bfloat16)

    sums = []
    for j in range(PIECES):
        scaled = jnp.stack([scaled_piece(z * share + j * width) for z in range(depth_count)])
        scaled = lax.optimization_barrier(scaled)
        sums.append(lax.psum_scatter(scaled, "depth", scatter_dimension=0))

    momenta, mine, squares = [], [], []
    for j in range(PIECES):
        gradient = sums[j]
        if mine:
            gradient, mine[-1] = lax.optimization_barrier((gradient, mine[-1]))
        gradient = gradient.astype(jnp.float32)
        new = BETA * lax.slice_in_dim(momentum, j * width, (j + 1) * width, axis=1) + gradient
        nesterov = gradient + BETA * new
        new, kept, square = lax.optimization_barrier(
            (new, nesterov.astype(jnp.bfloat16), jnp.sum(nesterov * nesterov))
        )
        momenta.append(new)
        mine.append(kept)
        squares.append(square)
    total_sq = lax.psum(sum(squares), ("row", "col", "depth"))
    factor = math.sqrt(M) / (1.5 * (jnp.sqrt(total_sq) + EPSILON))
    own = jnp.concatenate(mine, axis=1)

    product = None
    for j in range(PIECES):
        panel = lax.all_gather(mine[j], ("col", "depth"), axis=1, tiled=True)
        gram = lax.dot_general(
            panel, own, (((0,), (0,)), ((), ())), preferred_element_type=jnp.float32
        )
        gram = row_sum(gram.astype(jnp.bfloat16))
        gram = (gram * (factor * factor)).astype(jnp.bfloat16)
        term = jnp.dot(panel, gram, preferred_element_type=jnp.float32)
        product = term if product is None else product + term
    update = (math.sqrt(M) * factor) * (1.5 * own.astype(jnp.float32) - 0.5 * product)
    return (jnp.concatenate(momenta, axis=1), update)


def solution(mesh):
    placed = (P("depth", "row", "col"), P("depth", "row", "col"), P("row", ("col", "depth")))
    return jax.shard_map(
        body,
        mesh=mesh,
        in_specs=placed,
        out_specs=(P("row", ("col", "depth")), P("row", ("col", "depth"))),
        check_vma=False,
    )
```

```python
import functools
import math

import jax
import jax.numpy as jnp
from jax import lax
from jax.experimental import pallas as pl
from jax.experimental.pallas import tpu as pltpu
from jax.sharding import PartitionSpec as P

M = 8192
BETA = 0.95
EPSILON = 1e-07
PIECES = 4


def row_sum(block):
    if lax.axis_size("row") != 2:
        return lax.psum(block.astype(jnp.bfloat16), "row").astype(jnp.float32)
    moved = lax.ppermute(block.astype(jnp.bfloat16), "row", [(0, 1), (1, 0)])
    return block.astype(jnp.float32) + moved.astype(jnp.float32)


def after(value, earlier):
    return lax.optimization_barrier((value, earlier))[0]


def gather_pairs(block):
    middle = (lax.axis_index("depth") == 1) | (lax.axis_index("depth") == 2)
    outer = lax.ppermute(block, "depth", [(0, 1), (1, 0), (2, 3), (3, 2)])
    inner = lax.ppermute(block, "depth", [(1, 2), (2, 1)])
    far_inner = lax.ppermute(outer, "depth", [(1, 2), (2, 1)])
    far_outer = lax.ppermute(inner, "depth", [(2, 3), (1, 0)])
    last = lax.ppermute(far_inner, "depth", [(2, 3), (1, 0)])
    near = jnp.concatenate([block, outer], axis=1)
    far = jnp.concatenate(
        [jnp.where(middle, inner, far_outer), jnp.where(middle, far_inner, last)], axis=1
    )
    held = []
    for pair in (near, far):
        other = lax.ppermute(pair, "col", [(0, 2), (1, 3), (2, 0), (3, 1)])
        held += [pair, other]
    return (far, held[1]), held + [lax.ppermute(pair, "col", [(0, 1), (1, 0), (2, 3), (3, 2)]) for pair in held]


def gather(block):
    sizes = (lax.axis_size("row"), lax.axis_size("col"), lax.axis_size("depth"))
    if sizes == (2, 4, 4):
        return gather_pairs(block)
    return block, [lax.all_gather(block, ("col", "depth"), axis=1, tiled=True)]


def product_tile(summed, *refs):
    *parts, gram, out = refs[1:] if summed else refs
    width = parts[0].shape[1]
    total = refs[0][...] if summed else None
    for i, part in enumerate(parts):
        term = jnp.dot(
            part[...], gram[i * width : (i + 1) * width, :], preferred_element_type=jnp.float32
        )
        total = term if total is None else total + term
    out[...] = total


def add_product(running, parts, gram):
    rows, width = parts[0].shape
    columns = gram.shape[1]
    tile = min(rows, 256)
    summed = running is not None
    wide = pl.BlockSpec((tile, columns), lambda i: (i, 0))
    return pl.pallas_call(
        functools.partial(product_tile, summed),
        grid=(rows // tile,),
        out_shape=jax.ShapeDtypeStruct((rows, columns), jnp.float32),
        in_specs=[wide] * summed
        + [pl.BlockSpec((tile, width), lambda i: (i, 0))] * len(parts)
        + [pl.BlockSpec(gram.shape, lambda i: (0, 0))],
        out_specs=wide,
        input_output_aliases={0: 0} if summed else {},
        compiler_params=pltpu.CompilerParams(vmem_limit_bytes=32 * 2**20),
        cost_estimate=pl.CostEstimate(
            flops=2 * rows * gram.shape[0] * columns,
            bytes_accessed=2 * rows * gram.shape[0] + 8 * rows * columns,
            transcendentals=0,
        ),
    )(*([running] if summed else []), *parts, gram)


def body(grad_partial, grad_scale, momentum):
    depth_count = lax.axis_size("depth")
    rows_blk, cols_blk = grad_partial.shape[1:]
    share = cols_blk // depth_count
    width = share // PIECES
    groups = grad_scale.shape[1]
    group_rows = rows_blk // groups

    def scaled_piece(start):
        quant = lax.slice_in_dim(grad_partial[0], start, start + width, axis=1)
        scale = lax.slice_in_dim(grad_scale[0], start, start + width, axis=1)
        quant = quant.astype(jnp.float32).reshape(groups, group_rows, width)
        return (quant * scale[:, None, :]).reshape(rows_blk, width).astype(jnp.bfloat16)

    sums = []
    for j in range(PIECES):
        scaled = jnp.stack([scaled_piece(z * share + j * width) for z in range(depth_count)])
        scaled = lax.optimization_barrier(scaled)
        sums.append(lax.psum_scatter(scaled, "depth", scatter_dimension=0))

    momenta, mine, squares, panels = [], [], [], []
    relayed = None
    for j in range(PIECES):
        gradient = sums[j]
        if relayed is not None:
            gradient = after(gradient, relayed)
        gradient = gradient.astype(jnp.float32)
        new = BETA * lax.slice_in_dim(momentum, j * width, (j + 1) * width, axis=1) + gradient
        nesterov = gradient + BETA * new
        kept, square = lax.optimization_barrier(
            (nesterov.astype(jnp.bfloat16), jnp.sum(nesterov * nesterov))
        )
        momenta.append(new)
        mine.append(kept)
        squares.append(square)
        relayed, held = gather(kept)
        if panels:
            relayed = (relayed, panels[-1])
        panels.append(held)
    total_sq = lax.psum(sum(squares), ("row", "col", "depth"))
    factor = math.sqrt(M) / (1.5 * (jnp.sqrt(total_sq) + EPSILON))
    own = jnp.concatenate(mine, axis=1)

    product = None
    for j in range(PIECES):
        held = panels[j]
        gram = jnp.concatenate(
            [
                lax.dot_general(
                    part, own, (((0,), (0,)), ((), ())), preferred_element_type=jnp.float32
                ).astype(jnp.bfloat16)
                for part in held
            ],
            axis=0,
        )
        gram = row_sum(gram)
        gram = (gram * (factor * factor)).astype(jnp.bfloat16)
        product = add_product(product, held, gram)
    update = (math.sqrt(M) * factor) * (1.5 * own.astype(jnp.float32) - 0.5 * product)
    return (jnp.concatenate(momenta, axis=1), update)


def solution(mesh):
    placed = (P("depth", "row", "col"), P("depth", "row", "col"), P("row", ("col", "depth")))
    return jax.shard_map(
        body,
        mesh=mesh,
        in_specs=placed,
        out_specs=(P("row", ("col", "depth")), P("row", ("col", "depth"))),
        check_vma=False,
    )
```

```python
import functools
import math

import jax
import jax.numpy as jnp
from jax import lax
from jax.experimental import pallas as pl
from jax.experimental.pallas import tpu as pltpu
from jax.sharding import PartitionSpec as P

M = 8192
BETA = 0.95
EPSILON = 1e-07
PIECES = 4


def row_sum(block):
    if lax.axis_size("row") != 2:
        return lax.psum(block.astype(jnp.bfloat16), "row").astype(jnp.float32)
    moved = lax.ppermute(block.astype(jnp.bfloat16), "row", [(0, 1), (1, 0)])
    return block.astype(jnp.float32) + moved.astype(jnp.float32)


def after(value, earlier):
    return lax.optimization_barrier((value, earlier))[0]


def across(block):
    return lax.ppermute(block, "col", [(0, 2), (1, 3), (2, 0), (3, 1)])


def gather_pairs(block, earlier):
    depth_count = lax.axis_size("depth")
    pair = jnp.concatenate([block, across(block)], axis=1)
    line = lax.all_gather(block, "depth", axis=0)
    if earlier:
        line = after(line, earlier)
    place = lax.axis_index("depth")
    rest = jnp.concatenate(
        [
            lax.dynamic_index_in_dim(line, (place + k) % depth_count, 0, keepdims=False)
            for k in range(1, depth_count)
        ],
        axis=1,
    )
    held = [pair, rest, across(rest)]
    return held + [lax.ppermute(part, "col", [(0, 1), (1, 0), (2, 3), (3, 2)]) for part in held]


def gather(block, earlier):
    sizes = (lax.axis_size("row"), lax.axis_size("col"), lax.axis_size("depth"))
    if sizes == (2, 4, 4):
        return gather_pairs(block, earlier)
    return [lax.all_gather(block, ("col", "depth"), axis=1, tiled=True)]


def product_tile(summed, *refs):
    *parts, gram, out = refs[1:] if summed else refs
    total = refs[0][...] if summed else None
    start = 0
    for part in parts:
        stop = start + part.shape[1]
        term = jnp.dot(part[...], gram[start:stop, :], preferred_element_type=jnp.float32)
        total = term if total is None else total + term
        start = stop
    out[...] = total


def add_product(running, parts, gram):
    rows = parts[0].shape[0]
    columns = gram.shape[1]
    tile = min(rows, 256)
    summed = running is not None
    wide = pl.BlockSpec((tile, columns), lambda i: (i, 0))
    return pl.pallas_call(
        functools.partial(product_tile, summed),
        grid=(rows // tile,),
        out_shape=jax.ShapeDtypeStruct((rows, columns), jnp.float32),
        in_specs=[wide] * summed
        + [pl.BlockSpec((tile, part.shape[1]), lambda i: (i, 0)) for part in parts]
        + [pl.BlockSpec(gram.shape, lambda i: (0, 0))],
        out_specs=wide,
        input_output_aliases={0: 0} if summed else {},
        compiler_params=pltpu.CompilerParams(vmem_limit_bytes=32 * 2**20),
        cost_estimate=pl.CostEstimate(
            flops=2 * rows * gram.shape[0] * columns,
            bytes_accessed=2 * rows * gram.shape[0] + 8 * rows * columns,
            transcendentals=0,
        ),
    )(*([running] if summed else []), *parts, gram)


def body(grad_partial, grad_scale, momentum):
    depth_count = lax.axis_size("depth")
    rows_blk, cols_blk = grad_partial.shape[1:]
    share = cols_blk // depth_count
    width = share // PIECES
    groups = grad_scale.shape[1]
    group_rows = rows_blk // groups

    def scaled_piece(start):
        quant = lax.slice_in_dim(grad_partial[0], start, start + width, axis=1)
        scale = lax.slice_in_dim(grad_scale[0], start, start + width, axis=1)
        quant = quant.astype(jnp.float32).reshape(groups, group_rows, width)
        return (quant * scale[:, None, :]).reshape(rows_blk, width).astype(jnp.bfloat16)

    sums = []
    for j in range(PIECES):
        scaled = jnp.stack([scaled_piece(z * share + j * width) for z in range(depth_count)])
        scaled = lax.optimization_barrier(scaled)
        sums.append(lax.psum_scatter(scaled, "depth", scatter_dimension=0))

    momenta, mine, squares, panels = [], [], [], []
    for j in range(PIECES):
        gradient = sums[j]
        if mine:
            gradient, mine[-1] = lax.optimization_barrier((gradient, mine[-1]))
        gradient = gradient.astype(jnp.float32)
        new = BETA * lax.slice_in_dim(momentum, j * width, (j + 1) * width, axis=1) + gradient
        nesterov = gradient + BETA * new
        kept, square = lax.optimization_barrier(
            (nesterov.astype(jnp.bfloat16), jnp.sum(nesterov * nesterov))
        )
        momenta.append(new)
        mine.append(kept)
        squares.append(square)
    for j in range(PIECES):
        earlier = [held[2] for held in panels[-1:] if len(held) > 1]
        earlier += [held[3:] for held in panels[-2:-1] if len(held) > 1]
        panels.append(gather(mine[j], earlier))
    total_sq = lax.psum(sum(squares), ("row", "col", "depth"))
    factor = math.sqrt(M) / (1.5 * (jnp.sqrt(total_sq) + EPSILON))
    own = jnp.concatenate(mine, axis=1)

    product = None
    for j in range(PIECES):
        held = panels[j]
        gram = jnp.concatenate(
            [
                lax.dot_general(
                    part, own, (((0,), (0,)), ((), ())), preferred_element_type=jnp.float32
                ).astype(jnp.bfloat16)
                for part in held
            ],
            axis=0,
        )
        gram = row_sum(gram)
        gram = (gram * (factor * factor)).astype(jnp.bfloat16)
        product = add_product(product, held, gram)
    update = (math.sqrt(M) * factor) * (1.5 * own.astype(jnp.float32) - 0.5 * product)
    return (jnp.concatenate(momenta, axis=1), update)


def solution(mesh):
    placed = (P("depth", "row", "col"), P("depth", "row", "col"), P("row", ("col", "depth")))
    return jax.shard_map(
        body,
        mesh=mesh,
        in_specs=placed,
        out_specs=(P("row", ("col", "depth")), P("row", ("col", "depth"))),
        check_vma=False,
    )
```
